32 devices in a mesh: row: 8 (over z, x), grp: 4 (over y, core).
Axes of the slice: x: 2, y: 2, z: 4, core: 2. Of those that a mesh axis runs over, the one named last changes fastest.
Arguments:
- features: bfloat16 [32768, 256], P(('row', 'grp')), may hold values from -6 to 6
- weight: bfloat16 [256, 256], replicated, may hold values from -0.375 to 0.375
- cotangent: bfloat16 [32768, 256], P(('row', 'grp')), may hold values from -6 to 6
- adjacency_tiles: bfloat16 [2048, 128, 128], P(('row', 'grp')), may hold values from -0.25 to 0.25
- tile_rows: int32 [2048], P(('row', 'grp')), may hold values from 0 to 7
- tile_cols: int32 [2048], P(('row', 'grp')), may hold values from 0 to 31
- tile_counts: int32 [32], P(('row', 'grp')), may hold values from 1 to 64, 1024 in all
Outputs:
- activated: bfloat16 [32768, 256], P(('row', 'grp'))
- feature_grad: bfloat16 [32768, 256], P(('row', 'grp'))
- weight_grad: float32 [256, 256], replicated
The draws below stay inside these ranges and needn't reach their ends.
Inputs may be any that keep to these rules, and one draw needn't show every extreme that they name: `tile_counts`: some device has all 64 slots live.
All inputs are finite; a program needn't handle non-finite values.
Results may differ from the reference program's by a relative error of at most 0.009.
Values may be sent and summed in bfloat16 or wider, within the bound.
No kernel may reach another device: no remote copies, remote signals or barrier semaphores. Data moves between devices by JAX's collectives and lax.ppermute only.
A program may use at most 64 MiB of HBM per device.

```python
import math
import jax
import jax.numpy as jnp
import numpy as np
from jax import lax

HID = 256
TILE = 128
BLK_DEV = 8
MAXT = 64
GBLK = 32
NODES = 32768
SLOTS = 2048
N_ROW = 8
N_GRP = 4


def set_ends(array, own_key, least, top_value):
    extent = array.shape
    place = [jax.random.randint(jax.random.fold_in(own_key, axis), (), 0, extent[axis]) for axis in range(len(extent))]
    array = array.at[tuple(place)].set(least)
    longest = extent.index(max(extent))
    place[longest] = (place[longest] + 1) % extent[longest]
    return array.at[tuple(place)].set(top_value)


def block_scale(stream_key, dims, pieces, smallest, high):
    loudness, own = 1.0, jax.random.fold_in(stream_key, 6)
    for dim, blocks in pieces:
        heights = jnp.exp(jax.random.uniform(jax.random.fold_in(own, dim), (blocks,), jnp.float32, smallest / len(pieces), high / len(pieces)))
        loudness = loudness * jnp.repeat(heights, dims[dim] // blocks).reshape([-1 if axis == dim else 1 for axis in range(len(dims))])
    return loudness


def length_profile(count, total, most, skew):
    portions = [(1 << 20) // math.isqrt(standing ** skew) + 1 for standing in range(2, count + 1)]
    surplus, given = total - most - (count - 1), [1] * (count - 1)
    while surplus > 0:
        candidates = [i for i in range(count - 1) if given[i] < most]
        mass, budget = sum([portions[i] for i in candidates]), surplus
        for i in candidates:
            addition = min(most - given[i], max(1, budget * portions[i] // mass), surplus)
            given[i] = given[i] + addition
            surplus = surplus - addition
    return np.array([most] + given)


def ragged(key, count, total, reach, skew):
    if count == 2:
        one = jax.random.randint(key, (), max(1, total - reach), min(reach, total - 1) + 1)
        return jnp.stack([one, total - one])
    sizes = jnp.asarray(length_profile(count, total, reach, skew), jnp.int32)
    couples = (count - 1) // 2
    giver, sink = sizes[1:1 + 2 * couples:2], sizes[2:2 + 2 * couples:2]
    slack = jnp.minimum(giver - 1, reach - sink)
    moved = jax.random.randint(jax.random.fold_in(key, 1), (couples,), 0, 1 << 20) % (slack + 1)
    sizes = sizes.at[1:1 + 2 * couples:2].set(giver - moved).at[2:2 + 2 * couples:2].set(sink + moved)
    return sizes[jax.random.permutation(jax.random.fold_in(key, 2), count)]


def scatter_about(stream_key, dims, deviation, bound, shards=(), kind=jnp.bfloat16):
    level = block_scale(stream_key, dims, shards, -0.22, 0.18) if shards else 1.0
    drawn = jax.random.normal(stream_key, dims, jnp.float32) * deviation * level
    return jnp.minimum(jnp.maximum(drawn, -bound), bound).astype(kind)


def setup_inputs(seed: int = 0) -> dict:
    keys = jax.random.split(jax.random.key(seed), 8)
    return {
        "features": scatter_about(keys[0], (NODES, HID), 1.0, 6.0, ((0, 32),)),
        "weight": scatter_about(keys[1], (HID, HID), HID ** -0.5, 0.375),
        "cotangent": scatter_about(keys[2], (NODES, HID), 1.0, 6.0, ((0, 32),)),
        "adjacency_tiles": scatter_about(keys[3], (SLOTS, TILE, TILE), (TILE * MAXT // (2 * BLK_DEV)) ** -0.5, 0.25, ((0, 32),)),
        "tile_rows": set_ends(jax.random.randint(keys[4], (SLOTS,), 0, BLK_DEV), jax.random.fold_in(keys[4], 1), 0, BLK_DEV - 1).astype(jnp.int32),
        "tile_cols": set_ends(jax.random.randint(keys[5], (SLOTS,), 0, GBLK), jax.random.fold_in(keys[5], 1), 0, GBLK - 1).astype(jnp.int32),
        "tile_counts": ragged(keys[6], N_ROW * N_GRP, N_ROW * N_GRP * MAXT // 2, MAXT, 2).astype(jnp.int32),
    }


def reference(features, weight, cotangent, adjacency_tiles, tile_rows, tile_cols, tile_counts):
    projected = jnp.dot(features, weight, preferred_element_type=jnp.float32).astype(jnp.bfloat16)
    group_blocks = BLK_DEV * N_GRP
    group_nodes = group_blocks * TILE
    node_dev = BLK_DEV * TILE

    def group_work(row_id):
        start_node = (row_id * group_nodes).astype(jnp.int32)
        panels = lax.dynamic_slice_in_dim(projected, start_node, group_nodes, 0).reshape(group_blocks, TILE, HID)

        def device_work(total, member):
            device = (row_id * N_GRP + member).astype(jnp.int32)
            slot_first = (device * MAXT).astype(jnp.int32)
            tile_vals = lax.dynamic_slice_in_dim(adjacency_tiles, slot_first, MAXT, 0).astype(jnp.float32)
            row_index = lax.dynamic_slice_in_dim(tile_rows, slot_first, MAXT, 0)
            col_index = lax.dynamic_slice_in_dim(tile_cols, slot_first, MAXT, 0)
            live_mask = (jnp.arange(MAXT, dtype=jnp.int32) < tile_counts[device]).astype(jnp.float32)
            products = jnp.einsum('tik,tkj->tij', tile_vals, panels[col_index].astype(jnp.float32))
            products = products * live_mask[:, None, None]
            preact = jnp.zeros((BLK_DEV, TILE, HID), jnp.float32).at[row_index].add(products)
            own_cot = lax.dynamic_slice_in_dim(cotangent, (device * node_dev).astype(jnp.int32), node_dev, 0)
            own_cot = own_cot.reshape(BLK_DEV, TILE, HID).astype(jnp.float32)
            sigmoid_z = jax.nn.sigmoid(preact)
            activated = (preact * sigmoid_z).astype(jnp.bfloat16)
            slope = (own_cot * sigmoid_z * (1.0 + preact * (1.0 - sigmoid_z))).astype(jnp.bfloat16)
            contrib = jnp.einsum('tki,tkj->tij', tile_vals, slope[row_index].astype(jnp.float32))
            contrib = contrib * live_mask[:, None, None]
            partial_sum = jnp.zeros((group_blocks, TILE, HID), jnp.float32).at[col_index].add(contrib)
            return total + partial_sum.astype(jnp.bfloat16).astype(jnp.float32), activated

        panel_sum, activated = lax.scan(device_work, jnp.zeros((group_blocks, TILE, HID), jnp.float32), jnp.arange(N_GRP, dtype=jnp.int32))
        panel_grad = panel_sum.reshape(group_nodes, HID).astype(jnp.bfloat16)
        feature_grad = lax.dot_general(panel_grad, weight, (((1,), (1,)), ((), ())), preferred_element_type=jnp.float32).astype(jnp.bfloat16)
        group_feats = lax.dynamic_slice_in_dim(features, start_node, group_nodes, 0)
        weight_part = lax.dot_general(group_feats, panel_grad, (((0,), (0,)), ((), ())), preferred_element_type=jnp.float32)
        return activated.reshape(group_nodes, HID), feature_grad, weight_part

    activated, feature_grad, weight_parts = lax.map(group_work, jnp.arange(N_ROW, dtype=jnp.int32))
    return (activated.reshape(-1, HID), feature_grad.reshape(-1, HID), jnp.sum(weight_parts, axis=0))
```

```python
import functools

import jax
import jax.numpy as jnp
from jax import lax
from jax.experimental import pallas as pl
from jax.experimental.pallas import tpu as pltpu
from jax.sharding import PartitionSpec as P

TILE = 128
UNROLL = 4
F32 = jnp.float32
BF16 = jnp.bfloat16

SMEM = pl.BlockSpec(memory_space=pltpu.SMEM)
VMEM = pl.BlockSpec(memory_space=pltpu.VMEM)


def params(mib):
    return pltpu.CompilerParams(vmem_limit_bytes=mib << 20)


def prep_body(cats, blocks_dev, cnt_ref, rows_ref, cols_ref, me_ref, list_ref, offs_ref, pos):
    live = cnt_ref[0]
    me = me_ref[0]
    half = blocks_dev // 2
    if cats == 1:
        pad_col = 0
        pad_acc = me_ref[1]
    else:
        pad_col = 0
        pad_acc = half
    pad = (blocks_dev << 8) | (pad_col << 16) | (pad_acc << 23)
    for k in range(cats):
        pos[k] = 0

    def blank(i, carry):
        list_ref[i] = pad
        return carry

    lax.fori_loop(0, list_ref.shape[0], blank, 0)

    def category(s):
        col = cols_ref[s]
        if cats == 1:
            return 0, col, col
        rel = lax.bitwise_xor(col // blocks_dev, me)
        local = lax.rem(col, blocks_dev)
        part = local // half
        return rel * 2 + part, local, local - part * half

    def count(s, carry):
        k = category(s)[0]
        pos[k] = pos[k] + 1
        return carry

    lax.fori_loop(0, live, count, 0)
    group = jnp.int32(0)
    for k in range(cats):
        n = pos[k]
        offs_ref[k] = group
        pos[k] = group * UNROLL
        group = group + (n + UNROLL - 1) // UNROLL
    offs_ref[cats] = group

    def place(s, carry):
        k, local, acc = category(s)
        p = pos[k]
        pos[k] = p + 1
        list_ref[p] = s | (rows_ref[s] << 8) | (local << 16) | (acc << 23)
        return carry

    lax.fori_loop(0, live, place, 0)


def tile_of(e):
    return e & 255


def row_of(e):
    return (e >> 8) & 255


def col_of(e):
    return (e >> 16) & 127


def acc_of(e):
    return e >> 23


def rows_at(block, n=TILE):
    return pl.ds(pl.multiple_of(block * TILE, TILE), n)


def forward_groups(list_ref, lo, hi, tiles_ref, x_ref, acc, mask):
    def step(g, carry):
        es = [list_ref[g * UNROLL + u] for u in range(UNROLL)]
        ds = [
            jnp.dot(
                tiles_ref[tile_of(e)],
                x_ref[rows_at(col_of(e) & mask), :],
                preferred_element_type=F32,
            )
            for e in es
        ]
        for e, d in zip(es, ds):
            acc[row_of(e)] += d
        return carry

    lax.fori_loop(lo, hi, step, 0)


def backward_groups(list_ref, lo, hi, tiles_ref, s_ref, acc, row_mask, by_half):
    def step(g, carry):
        es = [list_ref[g * UNROLL + u] for u in range(UNROLL)]
        ds = [
            lax.dot_general(
                tiles_ref[tile_of(e)],
                s_ref[rows_at(row_of(e) & row_mask), :],
                (((0,), (0,)), ((), ())),
                preferred_element_type=F32,
            )
            for e in es
        ]
        for e, d in zip(es, ds):
            acc[acc_of(e)] += d
        return carry

    lax.fori_loop(lo, hi, step, 0)


def forward_body(phases, masks, final, blocks_dev, first, refs):
    refs = list(refs)
    list_ref, offs_ref, tiles_ref = refs[:3]
    refs = refs[3:]
    xs = refs[: len(phases)]
    refs = refs[len(phases):]
    if not first:
        acc_in = refs.pop(0)
    if final:
        w_ref, cot_ref, core_ref = refs[:3]
        act_ref, sw_ref, keep_ref, send_ref = refs[3:7]
        refs = refs[7:]
        acc, wg = refs
    else:
        acc_out = refs[0]
        acc = refs[1]
    if first:
        acc[...] = jnp.zeros_like(acc)
    else:
        acc[0:blocks_dev] = acc_in[...]
    for (lo, hi), x_ref, mask in zip(phases, xs, masks):
        forward_groups(list_ref, offs_ref[lo], offs_ref[hi], tiles_ref, x_ref, acc, mask)
    if not final:
        acc_out[...] = acc[0:blocks_dev]
        return
    hid = w_ref.shape[0]
    w = w_ref[...]
    step_blocks = 4
    for b in range(0, blocks_dev, step_blocks):
        n = step_blocks * TILE
        agg = acc[b:b + step_blocks].reshape(n, hid).astype(BF16)
        pre = jnp.dot(agg, w, preferred_element_type=F32)
        sig = jax.nn.sigmoid(pre)
        act_ref[b * TILE:b * TILE + n, :] = (pre * sig).astype(BF16)
        cot = cot_ref[b * TILE:b * TILE + n, :].astype(F32)
        slope = (cot * sig * (1.0 + pre * (1.0 - sig))).astype(BF16)
        sw_ref[b * TILE:b * TILE + n, :] = lax.dot_general(
            slope, w, (((1,), (1,)), ((), ())), preferred_element_type=F32
        ).astype(BF16)
        part = lax.dot_general(agg, slope, (((0,), (0,)), ((), ())), preferred_element_type=F32)
        if b == 0:
            wg[...] = part
        else:
            wg[...] += part
    rows = keep_ref.shape[0]
    core = core_ref[0]
    keep_ref[...] = wg[pl.ds(pl.multiple_of(core * rows, rows), rows), :]
    send_ref[...] = wg[pl.ds(pl.multiple_of((1 - core) * rows, rows), rows), :]


def forward(lst, offs, tiles, xs, phases, masks, acc=None, tail=None):
    hid = xs[0].shape[1]
    first = acc is None
    final = tail is not None
    blocks_dev = 8 if acc is None else acc.shape[0]
    if tail is not None:
        blocks_dev = tail[1].shape[0] // TILE
    args = [lst, offs, tiles, *xs] + ([] if first else [acc])
    specs = [SMEM, SMEM] + [VMEM] * (len(args) - 2)
    scratch = [pltpu.VMEM((blocks_dev + 1, TILE, hid), F32)]
    if final:
        args += list(tail)
        specs += [VMEM, VMEM, SMEM]
        nodes = blocks_dev * TILE
        out = (
            jax.ShapeDtypeStruct((nodes, hid), BF16),
            jax.ShapeDtypeStruct((nodes, hid), BF16),
            jax.ShapeDtypeStruct((hid // 2, hid), F32),
            jax.ShapeDtypeStruct((hid // 2, hid), F32),
        )
        out_specs = (VMEM,) * 4
        scratch.append(pltpu.VMEM((hid, hid), F32))
    else:
        out = jax.ShapeDtypeStruct((blocks_dev, TILE, hid), F32)
        out_specs = VMEM

    def body(*refs):
        forward_body(phases, masks, final, blocks_dev, first, refs)

    return pl.pallas_call(
        body,
        out_shape=out,
        in_specs=specs,
        out_specs=out_specs,
        scratch_shapes=scratch,
        compiler_params=params(24),
    )(*args)


def backward(lst, offs, tiles, sw, cats, half, extra=None, dtype=BF16):
    nodes, hid = sw.shape
    row_mask = nodes // TILE - 1
    args = [lst, offs, tiles, sw] + ([] if extra is None else [extra])
    specs = [SMEM, SMEM] + [VMEM] * (len(args) - 2)
    span = half * TILE

    def body(*refs):
        list_ref, offs_ref, tiles_ref, sw_ref = refs[:4]
        extra_ref = None if extra is None else refs[4]
        out_ref, acc = refs[-2:]
        for i, k in enumerate(cats):
            if extra_ref is None:
                acc[...] = jnp.zeros_like(acc)
            else:
                acc[0:half] = (
                    extra_ref[i * span:(i + 1) * span, :].astype(F32).reshape(half, TILE, hid)
                )
            backward_groups(
                list_ref, offs_ref[k], offs_ref[k + 1], tiles_ref, sw_ref, acc, row_mask, True
            )
            out_ref[i * span:(i + 1) * span, :] = acc[0:half].reshape(span, hid).astype(dtype)

    return pl.pallas_call(
        body,
        out_shape=jax.ShapeDtypeStruct((len(cats) * span, hid), dtype),
        in_specs=specs,
        out_specs=VMEM,
        scratch_shapes=[pltpu.VMEM((half + 1, TILE, hid), F32)],
        compiler_params=params(40 if half > 8 else 24),
    )(*args)


def prepare(tile_counts, tile_rows, tile_cols, me, group_blocks, cats, blocks_dev):
    slots = tile_rows.shape[0]
    length = (slots + cats * UNROLL + 31) // 32 * 32
    info = jnp.stack([me, jnp.int32(group_blocks)]).astype(jnp.int32)
    return pl.pallas_call(
        functools.partial(prep_body, cats, blocks_dev),
        out_shape=(
            jax.ShapeDtypeStruct((length,), jnp.int32),
            jax.ShapeDtypeStruct((cats + 1,), jnp.int32),
        ),
        in_specs=[SMEM] * 4,
        out_specs=(SMEM, SMEM),
        scratch_shapes=[pltpu.SMEM((cats,), jnp.int32)],
    )(tile_counts, tile_rows, tile_cols, info)


def local_four(row_size, features, weight, cotangent, tiles, tile_rows, tile_cols, tile_counts):
    nodes, hid = features.shape
    blocks_dev = nodes // TILE
    half = blocks_dev // 2
    cut = half * TILE
    me = lax.axis_index("grp").astype(jnp.int32)
    core = lax.bitwise_and(me, 1)

    def swap(x, bit):
        return lax.ppermute(x, "grp", [(i, i ^ bit) for i in range(4)])

    ya = swap(features[:cut], 2)
    yb = swap(features[cut:], 2)
    sib = swap(features, 1)
    lst, offs = prepare(tile_counts, tile_rows, tile_cols, me, 4 * blocks_dev, 8, blocks_dev)
    acc = forward(lst, offs, tiles, [features, sib], [(0, 2), (2, 4)], [7, 7])
    za = swap(ya, 1)
    zb = swap(yb, 1)
    acc = forward(lst, offs, tiles, [ya, za], [(4, 5), (6, 7)], [3, 3], acc)
    activated, sw, keep, send = forward(
        lst, offs, tiles, [yb, zb], [(5, 6), (7, 8)], [3, 3], acc,
        (weight, cotangent, core.reshape(1)),
    )
    p3 = backward(lst, offs, tiles, sw, (6, 7), half)
    r3 = swap(p3, 1)
    p1 = backward(lst, offs, tiles, sw, (2, 3), half)
    q = backward(lst, offs, tiles, sw, (4, 5), half, r3)
    qr = swap(q, 2)
    r1 = swap(p1, 1)
    p0 = backward(lst, offs, tiles, sw, (0, 1), half, r1, F32)
    feature_grad = (p0 + qr.astype(F32)).astype(BF16)

    w = keep + swap(send, 1)

    def fold(w, axis, size, bit):
        mine = w.astype(BF16)
        other = lax.ppermute(mine, axis, [(i, i ^ bit) for i in range(size)])
        return mine.astype(F32) + other.astype(F32)

    bit = 1
    while bit < row_size:
        w = fold(w, "row", row_size, bit)
        bit *= 2
    w = fold(w, "grp", 4, 2)
    other = swap(w, 1)
    weight_grad = jnp.where(
        core == 0, jnp.concatenate([w, other]), jnp.concatenate([other, w])
    )
    return activated, feature_grad, weight_grad


def local_any(features, weight, cotangent, tiles, tile_rows, tile_cols, tile_counts):
    nodes, hid = features.shape
    blocks_dev = nodes // TILE
    members = lax.axis_size("grp")
    group_blocks = blocks_dev * members
    me = lax.axis_index("grp").astype(jnp.int32)
    panel = lax.all_gather(features, "grp", axis=0, tiled=True)
    lst, offs = prepare(tile_counts, tile_rows, tile_cols, me, group_blocks, 1, blocks_dev)
    activated, sw, keep, send = forward(
        lst, offs, tiles, [panel], [(0, 1)], [127], None,
        (weight, cotangent, jnp.zeros((1,), jnp.int32)),
    )
    partial = backward(lst, offs, tiles, sw, (0,), group_blocks)
    feature_grad = lax.psum_scatter(partial, "grp", scatter_dimension=0, tiled=True)
    weight_grad = lax.psum(jnp.concatenate([keep, send]), ("row", "grp"))
    return activated, feature_grad, weight_grad


def solution(mesh):
    rows, members = mesh.shape["row"], mesh.shape["grp"]
    split = P(("row", "grp"))
    if members == 4 and rows & (rows - 1) == 0:
        local = functools.partial(local_four, rows)
    else:
        local = local_any
    return jax.shard_map(
        local,
        mesh=mesh,
        in_specs=(split, P(), split, split, split, split, split),
        out_specs=(split, split, P()),
        check_vma=False,
    )
```

```python
import functools

import jax
import jax.numpy as jnp
from jax import lax
from jax.experimental import pallas as pl
from jax.experimental.pallas import tpu as pltpu
from jax.sharding import PartitionSpec as P

TILE = 128
UNROLL = 4
F32 = jnp.float32
BF16 = jnp.bfloat16

SMEM = pl.BlockSpec(memory_space=pltpu.SMEM)
VMEM = pl.BlockSpec(memory_space=pltpu.VMEM)


def params(mib):
    return pltpu.CompilerParams(vmem_limit_bytes=mib << 20)


class Plan:
    def __init__(self, slots, cats, blocks_dev):
        self.slots, self.cats, self.blocks_dev = slots, cats, blocks_dev
        self.length = slots + cats * (UNROLL - 1)
        self.length = (self.length + UNROLL - 1) // UNROLL * UNROLL

    def bounds(self, list_ref, lo, hi):
        return list_ref[self.length + lo], list_ref[self.length + hi]


def prep_body(plan, pad_col, me_ref, cnt_ref, rows_ref, cols_ref, list_ref):
    me = me_ref[0]
    cats, blocks_dev = plan.cats, plan.blocks_dev
    pad = (blocks_dev << 8) | (pad_col << 16)
    live = cnt_ref[0]

    def category(col):
        if cats == 1:
            return 0, col
        return lax.bitwise_xor(col // blocks_dev, me) * 8, lax.rem(col, blocks_dev)

    def count(s, total):
        return total + (1 << category(cols_ref[s])[0])

    total = lax.fori_loop(0, live, count, jnp.int32(0))
    group = jnp.int32(0)
    places = jnp.int32(0)
    for k in range(cats):
        n = (total >> (8 * k)) & 255
        list_ref[plan.length + k] = group
        places = places + ((group * UNROLL) << (8 * k))
        group = group + (n + UNROLL - 1) // UNROLL
        for u in range(1, UNROLL):
            list_ref[lax.max(group * UNROLL - u, 0)] = pad
    list_ref[plan.length + cats] = group

    def place(s, places):
        shift, local = category(cols_ref[s])
        list_ref[(places >> shift) & 255] = s | (rows_ref[s] << 8) | (local << 16)
        return places + (1 << shift)

    lax.fori_loop(0, live, place, places)


def prepare(plan, pad_col, me, info):
    return pl.pallas_call(
        functools.partial(prep_body, plan, pad_col),
        out_shape=jax.ShapeDtypeStruct((plan.length + plan.cats + 1,), jnp.int32),
        in_specs=[SMEM] * 4,
        out_specs=SMEM,
    )(me.reshape(1), *info)


def tile_of(e):
    return e & 255


def row_of(e):
    return (e >> 8) & 255


def col_of(e):
    return e >> 16


def rows_at(block):
    return pl.ds(pl.multiple_of(block * TILE, TILE), TILE)


def tie(x, *others):
    return lax.optimization_barrier((x, *others))[0]


def forward_groups(list_ref, bounds, tiles_ref, x_ref, acc):
    last = x_ref.shape[0] // TILE - 1

    def step(g, carry):
        es = [list_ref[g * UNROLL + u] for u in range(UNROLL)]
        ds = [
            jnp.dot(
                tiles_ref[tile_of(e)],
                x_ref[rows_at(lax.min(col_of(e), last)), :],
                preferred_element_type=F32,
            )
            for e in es
        ]
        for e, d in zip(es, ds):
            acc[row_of(e)] += d
        return carry

    lax.fori_loop(*bounds, step, 0)


def backward_groups(list_ref, bounds, tiles_ref, s_ref, acc):
    last = s_ref.shape[0] // TILE - 1

    def step(g, carry):
        es = [list_ref[g * UNROLL + u] for u in range(UNROLL)]
        ds = [
            lax.dot_general(
                tiles_ref[tile_of(e)],
                s_ref[rows_at(lax.min(row_of(e), last)), :],
                (((0,), (0,)), ((), ())),
                preferred_element_type=F32,
            )
            for e in es
        ]
        for e, d in zip(es, ds):
            acc[col_of(e)] += d
        return carry

    lax.fori_loop(*bounds, step, 0)


def forward_body(plan, phases, final, first, refs):
    refs = list(refs)
    list_ref, tiles_ref = refs[:2]
    xs = refs[2:2 + len(phases)]
    refs = refs[2 + len(phases):]
    blocks_dev = plan.blocks_dev
    if not first:
        acc_in = refs.pop(0)
    if final:
        w_ref, cot_ref, core_ref, act_ref, sw_ref, keep_ref, send_ref, acc, wg = refs
    else:
        acc_out, acc = refs
    if first:
        acc[...] = jnp.zeros_like(acc)
    else:
        acc[0:blocks_dev] = acc_in[...]
    for k, x_ref in zip(phases, xs):
        forward_groups(list_ref, plan.bounds(list_ref, k, k + 1), tiles_ref, x_ref, acc)
    if not final:
        acc_out[...] = acc[0:blocks_dev]
        return
    hid = w_ref.shape[0]
    w = w_ref[...]
    step_blocks = 4 if blocks_dev % 4 == 0 else 1
    n = step_blocks * TILE
    for b in range(0, blocks_dev, step_blocks):
        at = slice(b * TILE, b * TILE + n)
        agg = acc[b:b + step_blocks].reshape(n, hid).astype(BF16)
        pre = jnp.dot(agg, w, preferred_element_type=F32)
        sig = jax.nn.sigmoid(pre)
        act_ref[at, :] = (pre * sig).astype(BF16)
        slope = (cot_ref[at, :].astype(F32) * sig * (1.0 + pre * (1.0 - sig))).astype(BF16)
        sw_ref[at, :] = lax.dot_general(
            slope, w, (((1,), (1,)), ((), ())), preferred_element_type=F32
        ).astype(BF16)
        part = lax.dot_general(agg, slope, (((0,), (0,)), ((), ())), preferred_element_type=F32)
        if b == 0:
            wg[...] = part
        else:
            wg[...] += part
    rows = keep_ref.shape[0]
    core = core_ref[0]
    keep_ref[...] = wg[pl.ds(pl.multiple_of(core * rows, rows), rows), :]
    send_ref[...] = wg[pl.ds(pl.multiple_of((1 - core) * rows, rows), rows), :]


def forward(plan, lst, tiles, xs, phases, acc=None, tail=None):
    hid = xs[0].shape[1]
    blocks_dev = plan.blocks_dev
    first, final = acc is None, tail is not None
    args = [lst, tiles, *xs] + ([] if first else [acc])
    specs = [SMEM] + [VMEM] * (len(args) - 1)
    scratch = [pltpu.VMEM((blocks_dev + 1, TILE, hid), F32)]
    if final:
        args += list(tail)
        specs += [VMEM, VMEM, SMEM]
        out = (
            jax.ShapeDtypeStruct((blocks_dev * TILE, hid), BF16),
            jax.ShapeDtypeStruct((blocks_dev * TILE, hid), BF16),
            jax.ShapeDtypeStruct((hid // 2, hid), F32),
            jax.ShapeDtypeStruct((hid // 2, hid), F32),
        )
        out_specs = (VMEM,) * 4
        scratch.append(pltpu.VMEM((hid, hid), F32))
    else:
        out = jax.ShapeDtypeStruct((blocks_dev, TILE, hid), F32)
        out_specs = VMEM

    def body(*refs):
        forward_body(plan, phases, final, first, refs)

    return pl.pallas_call(
        body,
        out_shape=out,
        in_specs=specs,
        out_specs=out_specs,
        scratch_shapes=scratch,
        compiler_params=params(12),
    )(*args)


def backward(plan, sources, blocks, extra=None, dtype=BF16):
    hid = sources[0][3].shape[1]
    args = [part for source in sources for part in source[1:]]
    specs = [SMEM, VMEM, VMEM] * len(sources)
    if extra is not None:
        args.append(extra)
        specs.append(VMEM)

    def body(*refs):
        out_ref, acc = refs[-2:]
        if extra is None:
            acc[...] = jnp.zeros_like(acc)
        else:
            acc[0:blocks] = refs[-3][...].astype(F32).reshape(blocks, TILE, hid)
        for i, source in enumerate(sources):
            list_ref, tiles_ref, s_ref = refs[3 * i:3 * i + 3]
            bounds = plan.bounds(list_ref, source[0], source[0] + 1)
            backward_groups(list_ref, bounds, tiles_ref, s_ref, acc)
        out_ref[...] = acc[0:blocks].reshape(blocks * TILE, hid).astype(dtype)

    return pl.pallas_call(
        body,
        out_shape=jax.ShapeDtypeStruct((blocks * TILE, hid), dtype),
        in_specs=specs,
        out_specs=VMEM,
        scratch_shapes=[pltpu.VMEM((blocks + 1, TILE, hid), F32)],
        compiler_params=params(40 if blocks > 8 else 12),
    )(*args)


def local_four(features, weight, cotangent, tiles, tile_rows, tile_cols, tile_counts):
    blocks_dev = features.shape[0] // TILE
    me = lax.axis_index("grp").astype(jnp.int32)
    core = lax.bitwise_and(me, 1)

    def swap(x, bit):
        return lax.ppermute(x, "grp", [(i, i ^ bit) for i in range(4)])

    def fold(w, axis, size, bit, *others):
        other = lax.ppermute(w, axis, [(i, i ^ bit) for i in range(size)])
        if others:
            other = tie(other, *others)
        return (w.astype(F32) + other.astype(F32)).astype(BF16)

    far = swap(features, 2)
    sib = swap(features, 1)
    plan = Plan(tile_rows.shape[0], 4, blocks_dev)
    lst = prepare(plan, blocks_dev, me, [tile_counts, tile_rows, tile_cols])
    acc = forward(plan, lst, tiles, [features, sib], [0, 1])
    far = tie(far, acc)
    diag = swap(far, 1)
    acc = forward(plan, lst, tiles, [far], [2], acc)
    activated, sw, keep, send = forward(
        plan, lst, tiles, [diag], [3], acc, (weight, cotangent, core.reshape(1))
    )

    def part(rel, sw, extra=None, dtype=BF16):
        return backward(plan, [(rel, lst, tiles, sw)], blocks_dev, extra, dtype)

    send = swap(send, 1)
    p3 = part(3, sw)
    r3 = swap(p3, 1)
    w = (keep + tie(send, p3)).astype(BF16)
    q = part(2, tie(sw, w), None, F32)
    q = (q + r3.astype(F32)).astype(BF16)
    q_far = swap(q, 2)
    w = fold(w, "grp", 4, 2, q)
    p1 = part(1, tie(sw, w))
    r1 = swap(p1, 1)
    w = fold(w, "row", 8, 1, p1)
    p0 = part(0, tie(sw, w), r1, F32)
    w = fold(w, "row", 8, 2, p0)
    w = fold(w, "row", 8, 4, q_far)
    other = swap(w, 1)
    weight_grad = jnp.where(
        core == 0, jnp.concatenate([w, other]), jnp.concatenate([other, w])
    ).astype(F32)
    feature_grad = (p0 + q_far.astype(F32)).astype(BF16)
    return activated, feature_grad, weight_grad


def local_any(features, weight, cotangent, tiles, tile_rows, tile_cols, tile_counts):
    blocks_dev = features.shape[0] // TILE
    group_blocks = blocks_dev * lax.axis_size("grp")
    me = lax.axis_index("grp").astype(jnp.int32)
    panel = lax.all_gather(features, "grp", axis=0, tiled=True)
    info = [tile_counts, tile_rows, tile_cols]
    plan = Plan(tile_rows.shape[0], 1, blocks_dev)
    lst = prepare(plan, group_blocks, me, info)
    activated, sw, keep, send = forward(
        plan, lst, tiles, [panel], [0], None, (weight, cotangent, jnp.zeros((1,), jnp.int32))
    )
    partial = backward(plan, [(0, lst, tiles, sw)], group_blocks)
    feature_grad = lax.psum_scatter(partial, "grp", scatter_dimension=0, tiled=True)
    weight_grad = lax.psum(jnp.concatenate([keep, send]), ("row", "grp"))
    return activated, feature_grad, weight_grad


def solution(mesh):
    split = P(("row", "grp"))
    four = mesh.shape["grp"] == 4 and mesh.shape["row"] == 8
    return jax.shard_map(
        local_four if four else local_any,
        mesh=mesh,
        in_specs=(split, P(), split, split, split, split, split),
        out_specs=(split, split, P()),
        check_vma=False,
    )
```

```python
import functools

import jax
import jax.numpy as jnp
from jax import lax
from jax.experimental import pallas as pl
from jax.experimental.pallas import tpu as pltpu
from jax.sharding import PartitionSpec as P

TILE = 128
UNROLL = 4
F32 = jnp.float32
BF16 = jnp.bfloat16

SMEM = pl.BlockSpec(memory_space=pltpu.SMEM)
VMEM = pl.BlockSpec(memory_space=pltpu.VMEM)


def params(mib):
    return pltpu.CompilerParams(vmem_limit_bytes=mib << 20)


class Plan:
    def __init__(self, slots, cats, blocks_dev):
        self.slots, self.cats, self.blocks_dev = slots, cats, blocks_dev
        self.length = slots + cats * (UNROLL - 1)
        self.length = (self.length + UNROLL - 1) // UNROLL * UNROLL

    def bounds(self, list_ref, lo, hi):
        return list_ref[self.length + lo], list_ref[self.length + hi]


def prep_body(plan, pad_col, me_ref, cnt_ref, rows_ref, cols_ref, list_ref):
    me = me_ref[0]
    cats, blocks_dev = plan.cats, plan.blocks_dev
    pad = (blocks_dev << 8) | (pad_col << 16)
    live = cnt_ref[0]

    def category(col):
        if cats == 1:
            return 0, col
        return lax.bitwise_xor(col // blocks_dev, me) * 8, lax.rem(col, blocks_dev)

    def count(s, total):
        return total + (1 << category(cols_ref[s])[0])

    total = lax.fori_loop(0, live, count, jnp.int32(0))
    group = jnp.int32(0)
    places = jnp.int32(0)
    for k in range(cats):
        n = (total >> (8 * k)) & 255
        list_ref[plan.length + k] = group
        places = places + ((group * UNROLL) << (8 * k))
        group = group + (n + UNROLL - 1) // UNROLL
        for u in range(1, UNROLL):
            list_ref[lax.max(group * UNROLL - u, 0)] = pad
    list_ref[plan.length + cats] = group

    def place(s, places):
        shift, local = category(cols_ref[s])
        list_ref[(places >> shift) & 255] = s | (rows_ref[s] << 8) | (local << 16)
        return places + (1 << shift)

    lax.fori_loop(0, live, place, places)


def prepare(plan, pad_col, me, info):
    return pl.pallas_call(
        functools.partial(prep_body, plan, pad_col),
        out_shape=jax.ShapeDtypeStruct((plan.length + plan.cats + 1,), jnp.int32),
        in_specs=[SMEM] * 4,
        out_specs=SMEM,
    )(me.reshape(1), *info)


def tile_of(e):
    return e & 255


def row_of(e):
    return (e >> 8) & 255


def col_of(e):
    return e >> 16


def rows_at(block):
    return pl.ds(pl.multiple_of(block * TILE, TILE), TILE)


def tie(x, *others):
    return lax.optimization_barrier((x, *others))[0]


def forward_groups(list_ref, bounds, tiles_ref, x_ref, acc):
    last = x_ref.shape[0] // TILE - 1

    def step(g, carry):
        es = [list_ref[g * UNROLL + u] for u in range(UNROLL)]
        ds = [
            jnp.dot(
                tiles_ref[tile_of(e)],
                x_ref[rows_at(lax.min(col_of(e), last)), :],
                preferred_element_type=F32,
            )
            for e in es
        ]
        for e, d in zip(es, ds):
            acc[row_of(e)] += d
        return carry

    lax.fori_loop(*bounds, step, 0)


def backward_groups(list_ref, bounds, tiles_ref, s_ref, acc):
    last = s_ref.shape[0] // TILE - 1

    def step(g, carry):
        es = [list_ref[g * UNROLL + u] for u in range(UNROLL)]
        ds = [
            lax.dot_general(
                tiles_ref[tile_of(e)],
                s_ref[rows_at(lax.min(row_of(e), last)), :],
                (((0,), (0,)), ((), ())),
                preferred_element_type=F32,
            )
            for e in es
        ]
        for e, d in zip(es, ds):
            acc[col_of(e)] += d
        return carry

    lax.fori_loop(*bounds, step, 0)


def forward_body(plan, phases, final, first, refs):
    refs = list(refs)
    list_ref, tiles_ref = refs[:2]
    xs = refs[2:2 + len(phases)]
    refs = refs[2 + len(phases):]
    blocks_dev = plan.blocks_dev
    if not first:
        acc_in = refs.pop(0)
    if final:
        w_ref, cot_ref, core_ref, act_ref, sw_ref, keep_ref, send_ref, acc, wg = refs
    else:
        acc_out, acc = refs
    if first:
        acc[...] = jnp.zeros_like(acc)
    else:
        acc[0:blocks_dev] = acc_in[...]
    for k, x_ref in zip(phases, xs):
        forward_groups(list_ref, plan.bounds(list_ref, k, k + 1), tiles_ref, x_ref, acc)
    if not final:
        acc_out[...] = acc[0:blocks_dev]
        return
    hid = w_ref.shape[0]
    w = w_ref[...]
    step_blocks = 4 if blocks_dev % 4 == 0 else 1
    n = step_blocks * TILE
    for b in range(0, blocks_dev, step_blocks):
        at = slice(b * TILE, b * TILE + n)
        agg = acc[b:b + step_blocks].reshape(n, hid).astype(BF16)
        pre = jnp.dot(agg, w, preferred_element_type=F32)
        sig = jax.nn.sigmoid(pre)
        act_ref[at, :] = (pre * sig).astype(BF16)
        slope = (cot_ref[at, :].astype(F32) * sig * (1.0 + pre * (1.0 - sig))).astype(BF16)
        sw_ref[at, :] = lax.dot_general(
            slope, w, (((1,), (1,)), ((), ())), preferred_element_type=F32
        ).astype(BF16)
        part = lax.dot_general(agg, slope, (((0,), (0,)), ((), ())), preferred_element_type=F32)
        if b == 0:
            wg[...] = part
        else:
            wg[...] += part
    rows = keep_ref.shape[0]
    core = core_ref[0]
    keep_ref[...] = wg[pl.ds(pl.multiple_of(core * rows, rows), rows), :]
    send_ref[...] = wg[pl.ds(pl.multiple_of((1 - core) * rows, rows), rows), :]


def forward(plan, lst, tiles, xs, phases, acc=None, tail=None):
    hid = xs[0].shape[1]
    blocks_dev = plan.blocks_dev
    first, final = acc is None, tail is not None
    args = [lst, tiles, *xs] + ([] if first else [acc])
    specs = [SMEM] + [VMEM] * (len(args) - 1)
    scratch = [pltpu.VMEM((blocks_dev + 1, TILE, hid), F32)]
    if final:
        args += list(tail)
        specs += [VMEM, VMEM, SMEM]
        out = (
            jax.ShapeDtypeStruct((blocks_dev * TILE, hid), BF16),
            jax.ShapeDtypeStruct((blocks_dev * TILE, hid), BF16),
            jax.ShapeDtypeStruct((hid // 2, hid), F32),
            jax.ShapeDtypeStruct((hid // 2, hid), F32),
        )
        out_specs = (VMEM,) * 4
        scratch.append(pltpu.VMEM((hid, hid), F32))
    else:
        out = jax.ShapeDtypeStruct((blocks_dev, TILE, hid), F32)
        out_specs = VMEM

    def body(*refs):
        forward_body(plan, phases, final, first, refs)

    return pl.pallas_call(
        body,
        out_shape=out,
        in_specs=specs,
        out_specs=out_specs,
        scratch_shapes=scratch,
        compiler_params=params(12),
    )(*args)


def backward(plan, sources, blocks, extra=None, dtype=BF16, us=0):
    hid = sources[0][3].shape[1]
    args = [part for source in sources for part in source[1:]]
    specs = [SMEM, VMEM, VMEM] * len(sources)
    if extra is not None:
        args.append(extra)
        specs.append(VMEM)

    def body(*refs):
        out_ref, acc = refs[-2:]
        if extra is None:
            acc[...] = jnp.zeros_like(acc)
        else:
            acc[0:blocks] = refs[-3][...].astype(F32).reshape(blocks, TILE, hid)
        for i, source in enumerate(sources):
            list_ref, tiles_ref, s_ref = refs[3 * i:3 * i + 3]
            bounds = plan.bounds(list_ref, source[0], source[0] + 1)
            backward_groups(list_ref, bounds, tiles_ref, s_ref, acc)
        out_ref[...] = acc[0:blocks].reshape(blocks * TILE, hid).astype(dtype)

    return pl.pallas_call(
        body,
        out_shape=jax.ShapeDtypeStruct((blocks * TILE, hid), dtype),
        in_specs=specs,
        out_specs=VMEM,
        scratch_shapes=[pltpu.VMEM((blocks + 1, TILE, hid), F32)],
        compiler_params=params(40 if blocks > 8 else 12),
        cost_estimate=pl.CostEstimate(
            flops=int(us * 1.1e9), bytes_accessed=1024, transcendentals=0
        ),
    )(*args)


def local_four(features, weight, cotangent, tiles, tile_rows, tile_cols, tile_counts):
    blocks_dev = features.shape[0] // TILE
    me = lax.axis_index("grp").astype(jnp.int32)
    core = lax.bitwise_and(me, 1)

    def swap(x, bit):
        return lax.ppermute(x, "grp", [(i, i ^ bit) for i in range(4)])

    def fold(w, axis, size, bit, *others):
        other = lax.ppermute(w, axis, [(i, i ^ bit) for i in range(size)])
        if others:
            other = tie(other, *others)
        return (w.astype(F32) + other.astype(F32)).astype(BF16)

    far = swap(features, 2)
    sib = swap(features, 1)
    plan = Plan(tile_rows.shape[0], 4, blocks_dev)
    lst = prepare(plan, blocks_dev, me, [tile_counts, tile_rows, tile_cols])
    acc = forward(plan, lst, tiles, [features, sib], [0, 1])
    far = tie(far, acc)
    diag = swap(far, 1)
    acc = forward(plan, lst, tiles, [far], [2], acc)
    activated, sw, keep, send = forward(
        plan, lst, tiles, [diag], [3], acc, (weight, cotangent, core.reshape(1))
    )

    def part(rel, sw, extra=None, dtype=BF16, us=0):
        return backward(plan, [(rel, lst, tiles, sw)], blocks_dev, extra, dtype, us)

    send = swap(send, 1)
    p3 = part(3, sw)
    r3 = swap(p3, 1)
    w = (keep + send).astype(BF16)
    q = part(2, tie(sw, w), None, F32, 10)
    q = (q + r3.astype(F32)).astype(BF16)
    q_far = swap(q, 2)
    w = fold(w, "grp", 4, 2, q)
    p0 = part(0, tie(sw, w), None, F32)
    w = fold(w, "row", 8, 1, p0)
    p1 = part(1, tie(sw, w))
    r1 = swap(p1, 1)
    w = fold(w, "row", 8, 2, p1)
    w = fold(w, "row", 8, 4, q_far)
    feature_grad = (p0 + r1.astype(F32) + q_far.astype(F32)).astype(BF16)
    other = tie(swap(w, 1), feature_grad)
    weight_grad = jnp.where(
        core == 0, jnp.concatenate([w, other]), jnp.concatenate([other, w])
    ).astype(F32)
    return activated, feature_grad, weight_grad


def local_any(features, weight, cotangent, tiles, tile_rows, tile_cols, tile_counts):
    blocks_dev = features.shape[0] // TILE
    group_blocks = blocks_dev * lax.axis_size("grp")
    me = lax.axis_index("grp").astype(jnp.int32)
    panel = lax.all_gather(features, "grp", axis=0, tiled=True)
    info = [tile_counts, tile_rows, tile_cols]
    plan = Plan(tile_rows.shape[0], 1, blocks_dev)
    lst = prepare(plan, group_blocks, me, info)
    activated, sw, keep, send = forward(
        plan, lst, tiles, [panel], [0], None, (weight, cotangent, jnp.zeros((1,), jnp.int32))
    )
    partial = backward(plan, [(0, lst, tiles, sw)], group_blocks)
    feature_grad = lax.psum_scatter(partial, "grp", scatter_dimension=0, tiled=True)
    weight_grad = lax.psum(jnp.concatenate([keep, send]), ("row", "grp"))
    return activated, feature_grad, weight_grad


def solution(mesh):
    split = P(("row", "grp"))
    four = mesh.shape["grp"] == 4 and mesh.shape["row"] == 8
    return jax.shard_map(
        local_four if four else local_any,
        mesh=mesh,
        in_specs=(split, P(), split, split, split, split, split),
        out_specs=(split, split, P()),
        check_vma=False,
    )
```

```python
import functools

import jax
import jax.numpy as jnp
from jax import lax
from jax.experimental import pallas as pl
from jax.experimental.pallas import tpu as pltpu
from jax.sharding import PartitionSpec as P

TILE = 128
UNROLL = 8
F32 = jnp.float32
BF16 = jnp.bfloat16

SMEM = pl.BlockSpec(memory_space=pltpu.SMEM)
VMEM = pl.BlockSpec(memory_space=pltpu.VMEM)


def params(mib):
    return pltpu.CompilerParams(vmem_limit_bytes=mib << 20)


class Plan:
    def __init__(self, slots, cats, blocks_dev):
        self.slots, self.cats, self.blocks_dev = slots, cats, blocks_dev
        self.length = slots + cats * (UNROLL - 1)
        self.length = (self.length + UNROLL - 1) // UNROLL * UNROLL

    def bounds(self, list_ref, lo, hi):
        return list_ref[self.length + lo], list_ref[self.length + hi]


def prep_body(plan, pad_col, me_ref, cnt_ref, rows_ref, cols_ref, list_ref):
    me = me_ref[0]
    cats, blocks_dev = plan.cats, plan.blocks_dev
    pad = (blocks_dev << 8) | (pad_col << 16)
    live = cnt_ref[0]

    def category(col):
        if cats == 1:
            return 0, col
        return lax.bitwise_xor(col // blocks_dev, me) * 8, lax.rem(col, blocks_dev)

    def count(s, total):
        return total + (1 << category(cols_ref[s])[0])

    total = lax.fori_loop(0, live, count, jnp.int32(0))
    group = jnp.int32(0)
    places = jnp.int32(0)
    for k in range(cats):
        n = (total >> (8 * k)) & 255
        list_ref[plan.length + k] = group
        places = places + ((group * UNROLL) << (8 * k))
        group = group + (n + UNROLL - 1) // UNROLL
        for u in range(1, UNROLL):
            list_ref[lax.max(group * UNROLL - u, 0)] = pad
    list_ref[plan.length + cats] = group

    def place(s, places):
        shift, local = category(cols_ref[s])
        list_ref[(places >> shift) & 255] = s | (rows_ref[s] << 8) | (local << 16)
        return places + (1 << shift)

    lax.fori_loop(0, live, place, places)


def prepare(plan, pad_col, me, info):
    return pl.pallas_call(
        functools.partial(prep_body, plan, pad_col),
        out_shape=jax.ShapeDtypeStruct((plan.length + plan.cats + 1,), jnp.int32),
        in_specs=[SMEM] * 4,
        out_specs=SMEM,
    )(me.reshape(1), *info)


def tile_of(e):
    return e & 255


def row_of(e):
    return (e >> 8) & 255


def col_of(e):
    return e >> 16


def rows_at(block):
    return pl.ds(pl.multiple_of(block * TILE, TILE), TILE)


def tie(x, *others):
    return lax.optimization_barrier((x, *others))[0]


def join(*xs):
    return lax.optimization_barrier(xs)


def move(x):
    def body(x_ref, out_ref, sem):
        copy = pltpu.make_async_copy(x_ref, out_ref, sem)
        copy.start()
        copy.wait()

    return pl.pallas_call(
        body,
        out_shape=jax.ShapeDtypeStruct(x.shape, x.dtype),
        in_specs=[VMEM],
        out_specs=pl.BlockSpec(memory_space=pl.ANY),
        scratch_shapes=[pltpu.SemaphoreType.DMA],
        cost_estimate=pl.CostEstimate(flops=0, bytes_accessed=1024, transcendentals=0),
        compiler_params=params(4),
    )(x)


def add_rows(total, *parts):
    shape = parts[0].shape

    def body(*refs):
        out_ref = refs[-1]
        acc = refs[0][0:shape[0], :]
        for ref in refs[1:-1]:
            acc = acc + ref[...].astype(F32)
        out_ref[...] = acc.astype(BF16)

    return pl.pallas_call(
        body,
        out_shape=jax.ShapeDtypeStruct(shape, BF16),
        in_specs=[VMEM] * (1 + len(parts)),
        out_specs=VMEM,
        cost_estimate=pl.CostEstimate(flops=0, bytes_accessed=1024, transcendentals=0),
        compiler_params=params(8),
    )(total, *parts)


def forward_groups(list_ref, bounds, tiles_ref, x_ref, acc):
    last = x_ref.shape[0] // TILE - 1

    def step(g, carry):
        es = [list_ref[g * UNROLL + u] for u in range(UNROLL)]
        ds = [
            jnp.dot(
                tiles_ref[tile_of(e)],
                x_ref[rows_at(lax.min(col_of(e), last)), :],
                preferred_element_type=F32,
            )
            for e in es
        ]
        for e, d in zip(es, ds):
            acc[row_of(e)] += d
        return carry

    lax.fori_loop(*bounds, step, 0)


def backward_groups(list_ref, bounds, tiles_ref, s_ref, acc):
    last = s_ref.shape[0] // TILE - 1

    def step(g, carry):
        es = [list_ref[g * UNROLL + u] for u in range(UNROLL)]
        ds = [
            lax.dot_general(
                tiles_ref[tile_of(e)],
                s_ref[rows_at(lax.min(row_of(e), last)), :],
                (((0,), (0,)), ((), ())),
                preferred_element_type=F32,
            )
            for e in es
        ]
        for e, d in zip(es, ds):
            acc[col_of(e)] += d
        return carry

    lax.fori_loop(*bounds, step, 0)


def forward_body(plan, phases, final, first, refs):
    refs = list(refs)
    list_ref, tiles_ref = refs[:2]
    xs = refs[2:2 + len(phases)]
    refs = refs[2 + len(phases):]
    blocks_dev = plan.blocks_dev
    if not first:
        acc_in = refs.pop(0)
    if final:
        w_ref, cot_ref, core_ref, act_ref, sw_ref, keep_ref, send_ref, acc, wg = refs
    else:
        (acc,) = refs
    if first:
        acc[...] = jnp.zeros_like(acc)
    else:
        acc[0:blocks_dev] = acc_in[0:blocks_dev]
    for k, x_ref in zip(phases, xs):
        forward_groups(list_ref, plan.bounds(list_ref, k, k + 1), tiles_ref, x_ref, acc)
    if not final:
        return
    hid = w_ref.shape[0]
    w = w_ref[...]
    step_blocks = 4 if blocks_dev % 4 == 0 else 1
    n = step_blocks * TILE
    for b in range(0, blocks_dev, step_blocks):
        at = slice(b * TILE, b * TILE + n)
        agg = acc[b:b + step_blocks].reshape(n, hid).astype(BF16)
        pre = jnp.dot(agg, w, preferred_element_type=F32)
        sig = 0.5 + 0.5 * jnp.tanh(0.5 * pre)
        act_ref[at, :] = (pre * sig).astype(BF16)
        slope = (cot_ref[at, :].astype(F32) * sig * (1.0 + pre * (1.0 - sig))).astype(BF16)
        sw_ref[at, :] = lax.dot_general(
            slope, w, (((1,), (1,)), ((), ())), preferred_element_type=F32
        ).astype(BF16)
        part = lax.dot_general(agg, slope, (((0,), (0,)), ((), ())), preferred_element_type=F32)
        if b == 0:
            wg[...] = part
        else:
            wg[...] += part
    rows = keep_ref.shape[0]
    core = core_ref[0]
    keep_ref[...] = wg[pl.ds(pl.multiple_of(core * rows, rows), rows), :]
    send_ref[...] = wg[pl.ds(pl.multiple_of((1 - core) * rows, rows), rows), :]


def forward(plan, lst, tiles, xs, phases, acc=None, tail=None):
    hid = xs[0].shape[1]
    blocks_dev = plan.blocks_dev
    first, final = acc is None, tail is not None
    args = [lst, tiles, *xs] + ([] if first else [acc])
    specs = [SMEM] + [VMEM] * (len(args) - 1)
    scratch = []
    if final:
        scratch.append(pltpu.VMEM((blocks_dev + 1, TILE, hid), F32))
        args += list(tail)
        specs += [VMEM, VMEM, SMEM]
        out = (
            pltpu.VMEM((blocks_dev * TILE, hid), BF16),
            jax.ShapeDtypeStruct((blocks_dev * TILE, hid), BF16),
            jax.ShapeDtypeStruct((hid // 2, hid), F32),
            jax.ShapeDtypeStruct((hid // 2, hid), F32),
        )
        out_specs = (VMEM,) * 4
        scratch.append(pltpu.VMEM((hid, hid), F32))
    else:
        out = jax.ShapeDtypeStruct((blocks_dev + 1, TILE, hid), F32)
        out_specs = VMEM

    def body(*refs):
        forward_body(plan, phases, final, first, refs)

    return pl.pallas_call(
        body,
        out_shape=out,
        in_specs=specs,
        out_specs=out_specs,
        scratch_shapes=scratch,
        compiler_params=params(12),
    )(*args)


def backward(plan, lst, rel, tiles, s, blocks, rounded=True, us=0):
    hid = s.shape[1]

    def body(list_ref, tiles_ref, s_ref, out_ref, acc=None):
        acc = acc if rounded else out_ref
        acc[...] = jnp.zeros_like(acc)
        bounds = plan.bounds(list_ref, rel, rel + 1)
        backward_groups(list_ref, bounds, tiles_ref, s_ref, acc)
        if rounded:
            out_ref[...] = acc[0:blocks].reshape(blocks * TILE, hid).astype(BF16)

    shape = (blocks + 1, TILE, hid)
    out = pl.pallas_call(
        body,
        out_shape=jax.ShapeDtypeStruct(
            (blocks * TILE, hid) if rounded else shape, BF16 if rounded else F32
        ),
        in_specs=[SMEM, VMEM, VMEM],
        out_specs=VMEM,
        scratch_shapes=[pltpu.VMEM(shape, F32)] if rounded else [],
        compiler_params=params(40 if blocks > 8 else 12),
        cost_estimate=pl.CostEstimate(
            flops=int(us * 1.1e9), bytes_accessed=1024, transcendentals=0
        ),
    )(lst, tiles, s)
    return out if rounded else out.reshape(-1, hid)


def local_four(features, weight, cotangent, tiles, tile_rows, tile_cols, tile_counts):
    blocks_dev = features.shape[0] // TILE
    me = lax.axis_index("grp").astype(jnp.int32)
    core = lax.bitwise_and(me, 1)

    def swap(x, bit):
        return lax.ppermute(x, "grp", [(i, i ^ bit) for i in range(4)])

    def fold(w, axis, size, bit, *others):
        other = lax.ppermute(w, axis, [(i, i ^ bit) for i in range(size)])
        if others:
            other = tie(other, *others)
        return (w.astype(F32) + other.astype(F32)).astype(BF16)

    far = swap(features, 2)
    sib = swap(features, 1)
    plan = Plan(tile_rows.shape[0], 4, blocks_dev)
    lst = prepare(plan, blocks_dev, me, [tile_counts, tile_rows, tile_cols])
    acc = forward(plan, lst, tiles, [features, sib], [0, 1])
    far, acc = join(far, acc)
    diag = swap(far, 1)
    acc = forward(plan, lst, tiles, [far], [2], acc)
    activated, sw, keep, send = forward(
        plan, lst, tiles, [diag], [3], acc, (weight, cotangent, core.reshape(1))
    )

    def part(rel, sw, rounded=True, us=0):
        return backward(plan, lst, rel, tiles, sw, blocks_dev, rounded, us)

    send = swap(send, 1)
    p3 = part(3, sw)
    r3 = swap(p3, 1)
    w = (keep + send).astype(BF16)
    q = part(2, tie(sw, w), False, 10)
    q = add_rows(q, r3)
    q_far = swap(q, 2)
    w = fold(w, "grp", 4, 2, q)
    p0 = part(0, tie(sw, w), False)
    w = fold(w, "row", 8, 1, p0)
    p1 = part(1, tie(sw, w))
    r1 = swap(p1, 1)
    w = fold(w, "row", 8, 2, p1)
    activated = move(tie(activated, w))
    w = fold(w, "row", 8, 4, activated, q_far)
    feature_grad = add_rows(p0, r1, q_far)
    w = tie(w, feature_grad)
    other = swap(w, 1)
    weight_grad = jnp.where(
        core == 0, jnp.concatenate([w, other]), jnp.concatenate([other, w])
    ).astype(F32)
    return activated, feature_grad, weight_grad


def local_any(features, weight, cotangent, tiles, tile_rows, tile_cols, tile_counts):
    blocks_dev = features.shape[0] // TILE
    group_blocks = blocks_dev * lax.axis_size("grp")
    me = lax.axis_index("grp").astype(jnp.int32)
    panel = lax.all_gather(features, "grp", axis=0, tiled=True)
    info = [tile_counts, tile_rows, tile_cols]
    plan = Plan(tile_rows.shape[0], 1, blocks_dev)
    lst = prepare(plan, group_blocks, me, info)
    activated, sw, keep, send = forward(
        plan, lst, tiles, [panel], [0], None, (weight, cotangent, jnp.zeros((1,), jnp.int32))
    )
    partial = backward(plan, lst, 0, tiles, sw, group_blocks)
    feature_grad = lax.psum_scatter(partial, "grp", scatter_dimension=0, tiled=True)
    weight_grad = lax.psum(jnp.concatenate([keep, send]), ("row", "grp"))
    return activated, feature_grad, weight_grad


def solution(mesh):
    split = P(("row", "grp"))
    four = mesh.shape["grp"] == 4 and mesh.shape["row"] == 8
    return jax.shard_map(
        local_four if four else local_any,
        mesh=mesh,
        in_specs=(split, P(), split, split, split, split, split),
        out_specs=(split, split, P()),
        check_vma=False,
    )
```

```python
import functools

import jax
import jax.numpy as jnp
from jax import lax
from jax.experimental import pallas as pl
from jax.experimental.pallas import tpu as pltpu
from jax.sharding import PartitionSpec as P

TILE = 128
UNROLL = 8
F32 = jnp.float32
BF16 = jnp.bfloat16

SMEM = pl.BlockSpec(memory_space=pltpu.SMEM)
VMEM = pl.BlockSpec(memory_space=pltpu.VMEM)


def params(mib):
    return pltpu.CompilerParams(vmem_limit_bytes=mib << 20)


class Plan:
    def __init__(self, slots, cats, blocks_dev):
        self.slots, self.cats, self.blocks_dev = slots, cats, blocks_dev
        self.length = slots + cats * (UNROLL - 1)
        self.length = (self.length + UNROLL - 1) // UNROLL * UNROLL

    def bounds(self, list_ref, lo, hi):
        return list_ref[self.length + lo], list_ref[self.length + hi]


def prep_body(plan, pad_col, me_ref, cnt_ref, rows_ref, cols_ref, list_ref):
    me = me_ref[0]
    cats, blocks_dev = plan.cats, plan.blocks_dev
    pad = (blocks_dev << 8) | (pad_col << 16)
    live = cnt_ref[0]

    def category(col):
        if cats == 1:
            return 0, col
        return lax.bitwise_xor(col // blocks_dev, me) * 8, lax.rem(col, blocks_dev)

    def count(s, total):
        return total + (1 << category(cols_ref[s])[0])

    total = lax.fori_loop(0, live, count, jnp.int32(0))
    group = jnp.int32(0)
    places = jnp.int32(0)
    for k in range(cats):
        n = (total >> (8 * k)) & 255
        list_ref[plan.length + k] = group
        places = places + ((group * UNROLL) << (8 * k))
        group = group + (n + UNROLL - 1) // UNROLL
        for u in range(1, UNROLL):
            list_ref[lax.max(group * UNROLL - u, 0)] = pad
    list_ref[plan.length + cats] = group
    list_ref[plan.length + cats + 1] = me if cats > 1 else 0

    def place(s, places):
        shift, local = category(cols_ref[s])
        list_ref[(places >> shift) & 255] = s | (rows_ref[s] << 8) | (local << 16)
        return places + (1 << shift)

    lax.fori_loop(0, live, place, places)


def prepare(plan, pad_col, me, info):
    return pl.pallas_call(
        functools.partial(prep_body, plan, pad_col),
        out_shape=pltpu.SMEM((plan.length + plan.cats + 2,), jnp.int32),
        in_specs=[SMEM] * 4,
        out_specs=SMEM,
    )(me.reshape(1), *info)


def tile_of(e):
    return e & 255


def row_of(e):
    return (e >> 8) & 255


def col_of(e):
    return e >> 16


def rows_at(block):
    return pl.ds(pl.multiple_of(block * TILE, TILE), TILE)


def tie(x, *others):
    return lax.optimization_barrier((x, *others))[0]


def join(*xs):
    return lax.optimization_barrier(xs)


def move(x):
    def body(x_ref, out_ref, sem):
        copy = pltpu.make_async_copy(x_ref, out_ref, sem)
        copy.start()
        copy.wait()

    return pl.pallas_call(
        body,
        out_shape=jax.ShapeDtypeStruct(x.shape, x.dtype),
        in_specs=[VMEM],
        out_specs=pl.BlockSpec(memory_space=pl.ANY),
        scratch_shapes=[pltpu.SemaphoreType.DMA],
        cost_estimate=pl.CostEstimate(flops=0, bytes_accessed=1024, transcendentals=0),
        compiler_params=params(4),
    )(x)


def add_rows(total, *parts):
    shape = parts[0].shape

    def body(*refs):
        out_ref = refs[-1]
        acc = refs[0][0:shape[0], :]
        for ref in refs[1:-1]:
            acc = acc + ref[...].astype(F32)
        out_ref[...] = acc.astype(BF16)

    return pl.pallas_call(
        body,
        out_shape=jax.ShapeDtypeStruct(shape, BF16),
        in_specs=[VMEM] * (1 + len(parts)),
        out_specs=VMEM,
        cost_estimate=pl.CostEstimate(flops=0, bytes_accessed=1024, transcendentals=0),
        compiler_params=params(8),
    )(total, *parts)


def forward_groups(list_ref, bounds, tiles_ref, x_ref, acc):
    last = x_ref.shape[0] // TILE - 1

    def step(g, carry):
        es = [list_ref[g * UNROLL + u] for u in range(UNROLL)]
        ds = [
            jnp.dot(
                tiles_ref[tile_of(e)],
                x_ref[rows_at(lax.min(col_of(e), last)), :],
                preferred_element_type=F32,
            )
            for e in es
        ]
        for e, d in zip(es, ds):
            acc[row_of(e)] += d
        return carry

    lax.fori_loop(*bounds, step, 0)


def backward_groups(list_ref, bounds, tiles_ref, s_ref, acc):
    last = s_ref.shape[0] // TILE - 1

    def step(g, carry):
        es = [list_ref[g * UNROLL + u] for u in range(UNROLL)]
        ds = [
            lax.dot_general(
                tiles_ref[tile_of(e)],
                s_ref[rows_at(lax.min(row_of(e), last)), :],
                (((0,), (0,)), ((), ())),
                preferred_element_type=F32,
            )
            for e in es
        ]
        for e, d in zip(es, ds):
            acc[col_of(e)] += d
        return carry

    lax.fori_loop(*bounds, step, 0)


def forward_body(plan, phases, final, first, refs):
    refs = list(refs)
    list_ref, tiles_ref = refs[:2]
    xs = refs[2:2 + len(phases)]
    refs = refs[2 + len(phases):]
    blocks_dev = plan.blocks_dev
    if not first:
        acc_in = refs.pop(0)
    if final:
        w_ref, cot_ref, act_ref, sw_ref, keep_ref, send_ref, acc, wg = refs
    else:
        (acc,) = refs
    if first:
        acc[...] = jnp.zeros_like(acc)
    else:
        acc[0:blocks_dev] = acc_in[0:blocks_dev]
    for k, x_ref in zip(phases, xs):
        forward_groups(list_ref, plan.bounds(list_ref, k, k + 1), tiles_ref, x_ref, acc)
    if not final:
        return
    hid = w_ref.shape[0]
    w = w_ref[...]
    step_blocks = blocks_dev
    n = step_blocks * TILE
    for b in range(0, blocks_dev, step_blocks):
        at = slice(b * TILE, b * TILE + n)
        agg = acc[b:b + step_blocks].reshape(n, hid).astype(BF16)
        pre = jnp.dot(agg, w, preferred_element_type=F32)
        sig = 0.5 + 0.5 * jnp.tanh(0.5 * pre)
        act_ref[at, :] = (pre * sig).astype(BF16)
        slope = (cot_ref[at, :].astype(F32) * sig * (1.0 + pre * (1.0 - sig))).astype(BF16)
        sw_ref[at, :] = lax.dot_general(
            slope, w, (((1,), (1,)), ((), ())), preferred_element_type=F32
        ).astype(BF16)
        part = lax.dot_general(agg, slope, (((0,), (0,)), ((), ())), preferred_element_type=F32)
        if b == 0:
            wg[...] = part
        else:
            wg[...] += part
    rows = keep_ref.shape[0]
    core = list_ref[plan.length + plan.cats + 1] & 1
    keep_ref[...] = wg[pl.ds(pl.multiple_of(core * rows, rows), rows), :]
    send_ref[...] = wg[pl.ds(pl.multiple_of((1 - core) * rows, rows), rows), :]


def forward(plan, lst, tiles, xs, phases, acc=None, tail=None):
    hid = xs[0].shape[1]
    blocks_dev = plan.blocks_dev
    first, final = acc is None, tail is not None
    args = [lst, tiles, *xs] + ([] if first else [acc])
    specs = [SMEM] + [VMEM] * (len(args) - 1)
    scratch = []
    if final:
        scratch.append(pltpu.VMEM((blocks_dev + 1, TILE, hid), F32))
        args += list(tail)
        specs += [VMEM, VMEM]
        out = (
            pltpu.VMEM((blocks_dev * TILE, hid), BF16),
            jax.ShapeDtypeStruct((blocks_dev * TILE, hid), BF16),
            jax.ShapeDtypeStruct((hid // 2, hid), F32),
            jax.ShapeDtypeStruct((hid // 2, hid), F32),
        )
        out_specs = (VMEM,) * 4
        scratch.append(pltpu.VMEM((hid, hid), F32))
    else:
        out = jax.ShapeDtypeStruct((blocks_dev + 1, TILE, hid), F32)
        out_specs = VMEM

    def body(*refs):
        forward_body(plan, phases, final, first, refs)

    return pl.pallas_call(
        body,
        out_shape=out,
        in_specs=specs,
        out_specs=out_specs,
        scratch_shapes=scratch,
        compiler_params=params(12),
    )(*args)


def backward(plan, lst, rel, tiles, s, blocks, rounded=True, us=0):
    hid = s.shape[1]

    def body(list_ref, tiles_ref, s_ref, out_ref, acc=None):
        acc = acc if rounded else out_ref
        acc[...] = jnp.zeros_like(acc)
        bounds = plan.bounds(list_ref, rel, rel + 1)
        backward_groups(list_ref, bounds, tiles_ref, s_ref, acc)
        if rounded:
            out_ref[...] = acc[0:blocks].reshape(blocks * TILE, hid).astype(BF16)

    shape = (blocks + 1, TILE, hid)
    out = pl.pallas_call(
        body,
        out_shape=jax.ShapeDtypeStruct(
            (blocks * TILE, hid) if rounded else shape, BF16 if rounded else F32
        ),
        in_specs=[SMEM, VMEM, VMEM],
        out_specs=VMEM,
        scratch_shapes=[pltpu.VMEM(shape, F32)] if rounded else [],
        compiler_params=params(40 if blocks > 8 else 12),
        cost_estimate=pl.CostEstimate(
            flops=int(us * 1.1e9), bytes_accessed=1024, transcendentals=0
        ),
    )(lst, tiles, s)
    return out if rounded else out.reshape(-1, hid)


def local_four(features, weight, cotangent, tiles, tile_rows, tile_cols, tile_counts):
    blocks_dev = features.shape[0] // TILE
    me = lax.axis_index("grp").astype(jnp.int32)
    core = lax.bitwise_and(me, 1)

    def swap(x, bit):
        return lax.ppermute(x, "grp", [(i, i ^ bit) for i in range(4)])

    def fold(w, axis, size, bit, *others):
        other = lax.ppermute(w, axis, [(i, i ^ bit) for i in range(size)])
        if others:
            other = tie(other, *others)
        return (w.astype(F32) + other.astype(F32)).astype(BF16)

    far = swap(features, 2)
    sib = swap(features, 1)
    plan = Plan(tile_rows.shape[0], 4, blocks_dev)
    lst = prepare(plan, blocks_dev, me, [tile_counts, tile_rows, tile_cols])
    acc = forward(plan, lst, tiles, [features, sib], [0, 1])
    far, acc = join(far, acc)
    diag = swap(far, 1)
    acc = forward(plan, lst, tiles, [far], [2], acc)
    activated, sw, keep, send = forward(
        plan, lst, tiles, [diag], [3], acc, (weight, cotangent)
    )

    def part(rel, sw, rounded=True, us=0):
        return backward(plan, lst, rel, tiles, sw, blocks_dev, rounded, us)

    send = swap(send, 1)
    p3 = part(3, sw)
    r3 = swap(p3, 1)
    w = (keep + send).astype(BF16)
    q = part(2, tie(sw, w), False, 10)
    q = add_rows(q, r3)
    q_far = swap(q, 2)
    w = fold(w, "grp", 4, 2, q)
    p1 = part(1, tie(sw, w))
    w = fold(w, "row", 8, 1, p1)
    r1 = swap(tie(p1, w), 1)
    p0 = part(0, tie(sw, w), False)
    w = fold(w, "row", 8, 2, p0)
    activated = move(tie(activated, w))
    feature_grad = add_rows(p0, r1, q_far)
    w = fold(w, "row", 8, 4, activated, feature_grad)
    other = swap(w, 1)
    weight_grad = jnp.where(
        core == 0, jnp.concatenate([w, other]), jnp.concatenate([other, w])
    ).astype(F32)
    return activated, feature_grad, weight_grad


def local_any(features, weight, cotangent, tiles, tile_rows, tile_cols, tile_counts):
    blocks_dev = features.shape[0] // TILE
    group_blocks = blocks_dev * lax.axis_size("grp")
    me = lax.axis_index("grp").astype(jnp.int32)
    panel = lax.all_gather(features, "grp", axis=0, tiled=True)
    info = [tile_counts, tile_rows, tile_cols]
    plan = Plan(tile_rows.shape[0], 1, blocks_dev)
    lst = prepare(plan, group_blocks, me, info)
    activated, sw, keep, send = forward(
        plan, lst, tiles, [panel], [0], None, (weight, cotangent)
    )
    partial = backward(plan, lst, 0, tiles, sw, group_blocks)
    feature_grad = lax.psum_scatter(partial, "grp", scatter_dimension=0, tiled=True)
    weight_grad = lax.psum(jnp.concatenate([keep, send]), ("row", "grp"))
    return activated, feature_grad, weight_grad


def solution(mesh):
    split = P(("row", "grp"))
    four = mesh.shape["grp"] == 4 and mesh.shape["row"] == 8
    return jax.shard_map(
        local_four if four else local_any,
        mesh=mesh,
        in_specs=(split, P(), split, split, split, split, split),
        out_specs=(split, split, P()),
        check_vma=False,
    )
```

```python
import functools

import jax
import jax.numpy as jnp
from jax import lax
from jax.experimental import pallas as pl
from jax.experimental.pallas import tpu as pltpu
from jax.sharding import PartitionSpec as P

TILE = 128
UNROLL = 16
F32 = jnp.float32
BF16 = jnp.bfloat16

SMEM = pl.BlockSpec(memory_space=pltpu.SMEM)
VMEM = pl.BlockSpec(memory_space=pltpu.VMEM)


def params(mib):
    return pltpu.CompilerParams(vmem_limit_bytes=mib << 20)


class Plan:
    def __init__(self, slots, cats, blocks_dev):
        self.slots, self.cats, self.blocks_dev = slots, cats, blocks_dev
        self.length = slots + cats * (UNROLL - 1)
        self.length = (self.length + UNROLL - 1) // UNROLL * UNROLL

    def bounds(self, list_ref, lo, hi):
        return list_ref[self.length + lo], list_ref[self.length + hi]


def prep_body(plan, pad_col, me_ref, cnt_ref, rows_ref, cols_ref, list_ref):
    me = me_ref[0]
    cats, blocks_dev = plan.cats, plan.blocks_dev
    pad = (blocks_dev << 8) | (pad_col << 16)
    live = cnt_ref[0]

    def category(col):
        if cats == 1:
            return 0, col
        return lax.bitwise_xor(col // blocks_dev, me) * 8, lax.rem(col, blocks_dev)

    def count(s, total):
        return total + (1 << category(cols_ref[s])[0])

    total = lax.fori_loop(0, live, count, jnp.int32(0))
    group = jnp.int32(0)
    places = jnp.int32(0)
    for k in range(cats):
        n = (total >> (8 * k)) & 255
        list_ref[plan.length + k] = group
        places = places + ((group * UNROLL) << (8 * k))
        group = group + (n + UNROLL - 1) // UNROLL
        for u in range(1, UNROLL):
            list_ref[lax.max(group * UNROLL - u, 0)] = pad
    list_ref[plan.length + cats] = group
    list_ref[plan.length + cats + 1] = me if cats > 1 else 0

    def place(s, places):
        shift, local = category(cols_ref[s])
        list_ref[(places >> shift) & 255] = s | (rows_ref[s] << 8) | (local << 16)
        return places + (1 << shift)

    lax.fori_loop(0, live, place, places)


def prepare(plan, pad_col, me, info):
    return pl.pallas_call(
        functools.partial(prep_body, plan, pad_col),
        out_shape=pltpu.SMEM((plan.length + plan.cats + 2,), jnp.int32),
        in_specs=[SMEM] * 4,
        out_specs=SMEM,
    )(me.reshape(1), *info)


def tile_of(e):
    return e & 255


def row_of(e):
    return (e >> 8) & 255


def col_of(e):
    return e >> 16


def rows_at(block):
    return pl.ds(pl.multiple_of(block * TILE, TILE), TILE)


def tie(x, *others):
    return lax.optimization_barrier((x, *others))[0]


def join(*xs):
    return lax.optimization_barrier(xs)


def move(x):
    def body(x_ref, out_ref, sem):
        copy = pltpu.make_async_copy(x_ref, out_ref, sem)
        copy.start()
        copy.wait()

    return pl.pallas_call(
        body,
        out_shape=jax.ShapeDtypeStruct(x.shape, x.dtype),
        in_specs=[VMEM],
        out_specs=pl.BlockSpec(memory_space=pl.ANY),
        scratch_shapes=[pltpu.SemaphoreType.DMA],
        cost_estimate=pl.CostEstimate(flops=0, bytes_accessed=1024, transcendentals=0),
        compiler_params=params(4),
    )(x)


def add_rows(total, *parts):
    shape = parts[0].shape

    def body(*refs):
        out_ref = refs[-1]
        acc = refs[0][0:shape[0], :]
        for ref in refs[1:-1]:
            acc = acc + ref[...].astype(F32)
        out_ref[...] = acc.astype(BF16)

    return pl.pallas_call(
        body,
        out_shape=jax.ShapeDtypeStruct(shape, BF16),
        in_specs=[VMEM] * (1 + len(parts)),
        out_specs=VMEM,
        cost_estimate=pl.CostEstimate(flops=0, bytes_accessed=1024, transcendentals=0),
        compiler_params=params(8),
    )(total, *parts)


def forward_groups(list_ref, bounds, tiles_ref, x_ref, acc):
    last = x_ref.shape[0] // TILE - 1

    def step(g, carry):
        es = [list_ref[g * UNROLL + u] for u in range(UNROLL)]
        ds = [
            jnp.dot(
                tiles_ref[tile_of(e)],
                x_ref[rows_at(lax.min(col_of(e), last)), :],
                preferred_element_type=F32,
            )
            for e in es
        ]
        for e, d in zip(es, ds):
            acc[row_of(e)] += d
        return carry

    lax.fori_loop(*bounds, step, 0)


def backward_groups(list_ref, bounds, tiles_ref, s_ref, acc):
    last = s_ref.shape[0] // TILE - 1

    def step(g, carry):
        es = [list_ref[g * UNROLL + u] for u in range(UNROLL)]
        ds = [
            lax.dot_general(
                tiles_ref[tile_of(e)],
                s_ref[rows_at(lax.min(row_of(e), last)), :],
                (((0,), (0,)), ((), ())),
                preferred_element_type=F32,
            )
            for e in es
        ]
        for e, d in zip(es, ds):
            acc[col_of(e)] += d
        return carry

    lax.fori_loop(*bounds, step, 0)


def forward_body(plan, phases, final, first, refs):
    refs = list(refs)
    list_ref, tiles_ref = refs[:2]
    xs = refs[2:2 + len(phases)]
    refs = refs[2 + len(phases):]
    blocks_dev = plan.blocks_dev
    if not first:
        acc_in = refs.pop(0)
    if final:
        w_ref, cot_ref, act_ref, sw_ref, keep_ref, send_ref, acc, wg = refs
    else:
        (acc,) = refs
    if first:
        acc[...] = jnp.zeros_like(acc)
    else:
        acc[0:blocks_dev] = acc_in[0:blocks_dev]
    for k, x_ref in zip(phases, xs):
        forward_groups(list_ref, plan.bounds(list_ref, k, k + 1), tiles_ref, x_ref, acc)
    if not final:
        return
    hid = w_ref.shape[0]
    w = w_ref[...]
    step_blocks = blocks_dev
    n = step_blocks * TILE
    for b in range(0, blocks_dev, step_blocks):
        at = slice(b * TILE, b * TILE + n)
        agg = acc[b:b + step_blocks].reshape(n, hid).astype(BF16)
        pre = jnp.dot(agg, w, preferred_element_type=F32)
        sig = 0.5 + 0.5 * jnp.tanh(0.5 * pre)
        act_ref[at, :] = (pre * sig).astype(BF16)
        slope = (cot_ref[at, :].astype(F32) * sig * (1.0 + pre * (1.0 - sig))).astype(BF16)
        sw_ref[at, :] = lax.dot_general(
            slope, w, (((1,), (1,)), ((), ())), preferred_element_type=F32
        ).astype(BF16)
        part = lax.dot_general(agg, slope, (((0,), (0,)), ((), ())), preferred_element_type=F32)
        if b == 0:
            wg[...] = part
        else:
            wg[...] += part
    rows = keep_ref.shape[0]
    core = list_ref[plan.length + plan.cats + 1] & 1
    keep_ref[...] = wg[pl.ds(pl.multiple_of(core * rows, rows), rows), :]
    send_ref[...] = wg[pl.ds(pl.multiple_of((1 - core) * rows, rows), rows), :]


def forward(plan, lst, tiles, xs, phases, acc=None, tail=None):
    hid = xs[0].shape[1]
    blocks_dev = plan.blocks_dev
    first, final = acc is None, tail is not None
    args = [lst, tiles, *xs] + ([] if first else [acc])
    specs = [SMEM] + [VMEM] * (len(args) - 1)
    scratch = []
    if final:
        scratch.append(pltpu.VMEM((blocks_dev + 1, TILE, hid), F32))
        args += list(tail)
        specs += [VMEM, VMEM]
        out = (
            pltpu.VMEM((blocks_dev * TILE, hid), BF16),
            jax.ShapeDtypeStruct((blocks_dev * TILE, hid), BF16),
            jax.ShapeDtypeStruct((hid // 2, hid), F32),
            jax.ShapeDtypeStruct((hid // 2, hid), F32),
        )
        out_specs = (VMEM,) * 4
        scratch.append(pltpu.VMEM((hid, hid), F32))
    else:
        out = jax.ShapeDtypeStruct((blocks_dev + 1, TILE, hid), F32)
        out_specs = VMEM

    def body(*refs):
        forward_body(plan, phases, final, first, refs)

    return pl.pallas_call(
        body,
        out_shape=out,
        in_specs=specs,
        out_specs=out_specs,
        scratch_shapes=scratch,
        compiler_params=params(12),
    )(*args)


def backward(plan, lst, rel, tiles, s, blocks, rounded=True, us=0):
    hid = s.shape[1]

    def body(list_ref, tiles_ref, s_ref, out_ref, acc=None):
        acc = acc if rounded else out_ref
        acc[...] = jnp.zeros_like(acc)
        bounds = plan.bounds(list_ref, rel, rel + 1)
        backward_groups(list_ref, bounds, tiles_ref, s_ref, acc)
        if rounded:
            out_ref[...] = acc[0:blocks].reshape(blocks * TILE, hid).astype(BF16)

    shape = (blocks + 1, TILE, hid)
    out = pl.pallas_call(
        body,
        out_shape=jax.ShapeDtypeStruct(
            (blocks * TILE, hid) if rounded else shape, BF16 if rounded else F32
        ),
        in_specs=[SMEM, VMEM, VMEM],
        out_specs=VMEM,
        scratch_shapes=[pltpu.VMEM(shape, F32)] if rounded else [],
        compiler_params=params(40 if blocks > 8 else 12),
        cost_estimate=pl.CostEstimate(
            flops=int(us * 1.1e9), bytes_accessed=1024, transcendentals=0
        ),
    )(lst, tiles, s)
    return out if rounded else out.reshape(-1, hid)


def local_four(features, weight, cotangent, tiles, tile_rows, tile_cols, tile_counts):
    blocks_dev = features.shape[0] // TILE
    me = lax.axis_index("grp").astype(jnp.int32)
    core = lax.bitwise_and(me, 1)

    def swap(x, bit):
        return lax.ppermute(x, "grp", [(i, i ^ bit) for i in range(4)])

    def fold(w, axis, size, bit, *others):
        other = lax.ppermute(w, axis, [(i, i ^ bit) for i in range(size)])
        if others:
            other = tie(other, *others)
        return (w.astype(F32) + other.astype(F32)).astype(BF16)

    far = swap(features, 2)
    sib = swap(features, 1)
    plan = Plan(tile_rows.shape[0], 4, blocks_dev)
    lst = prepare(plan, blocks_dev, me, [tile_counts, tile_rows, tile_cols])
    acc = forward(plan, lst, tiles, [features, sib], [0, 1])
    far, acc = join(far, acc)
    diag = swap(far, 1)
    acc = forward(plan, lst, tiles, [far], [2], acc)
    activated, sw, keep, send = forward(
        plan, lst, tiles, [diag], [3], acc, (weight, cotangent)
    )

    def part(rel, sw, rounded=True, us=0):
        return backward(plan, lst, rel, tiles, sw, blocks_dev, rounded, us)

    send = swap(send, 1)
    p3 = part(3, sw)
    r3 = swap(p3, 1)
    w = (keep + send).astype(BF16)
    q = part(2, tie(sw, w), False, 10)
    q = add_rows(q, r3)
    q_far = swap(q, 2)
    w = fold(w, "grp", 4, 2, q)
    p1 = part(1, tie(sw, w))
    w = fold(w, "row", 8, 1, p1)
    r1 = swap(tie(p1, w), 1)
    p0 = part(0, tie(sw, w), False)
    w = fold(w, "row", 8, 2, p0)
    activated = move(tie(activated, w))
    feature_grad = add_rows(p0, r1, q_far)
    w = fold(w, "row", 8, 4, activated, feature_grad)
    other = swap(w, 1)
    weight_grad = jnp.where(
        core == 0, jnp.concatenate([w, other]), jnp.concatenate([other, w])
    ).astype(F32)
    return activated, feature_grad, weight_grad


def local_any(features, weight, cotangent, tiles, tile_rows, tile_cols, tile_counts):
    blocks_dev = features.shape[0] // TILE
    group_blocks = blocks_dev * lax.axis_size("grp")
    me = lax.axis_index("grp").astype(jnp.int32)
    panel = lax.all_gather(features, "grp", axis=0, tiled=True)
    info = [tile_counts, tile_rows, tile_cols]
    plan = Plan(tile_rows.shape[0], 1, blocks_dev)
    lst = prepare(plan, group_blocks, me, info)
    activated, sw, keep, send = forward(
        plan, lst, tiles, [panel], [0], None, (weight, cotangent)
    )
    partial = backward(plan, lst, 0, tiles, sw, group_blocks)
    feature_grad = lax.psum_scatter(partial, "grp", scatter_dimension=0, tiled=True)
    weight_grad = lax.psum(jnp.concatenate([keep, send]), ("row", "grp"))
    return activated, feature_grad, weight_grad


def solution(mesh):
    split = P(("row", "grp"))
    four = mesh.shape["grp"] == 4 and mesh.shape["row"] == 8
    return jax.shard_map(
        local_four if four else local_any,
        mesh=mesh,
        in_specs=(split, P(), split, split, split, split, split),
        out_specs=(split, split, P()),
        check_vma=False,
    )
```

```python
import functools

import jax
import jax.numpy as jnp
from jax import lax
from jax.experimental import pallas as pl
from jax.experimental.pallas import tpu as pltpu
from jax.sharding import PartitionSpec as P

TILE = 128
UNROLL = 16
F32 = jnp.float32
BF16 = jnp.bfloat16

SMEM = pl.BlockSpec(memory_space=pltpu.SMEM)
VMEM = pl.BlockSpec(memory_space=pltpu.VMEM)


def params(mib):
    return pltpu.CompilerParams(vmem_limit_bytes=mib << 20)


class Plan:
    def __init__(self, slots, cats, blocks_dev):
        self.slots, self.cats, self.blocks_dev = slots, cats, blocks_dev
        self.length = slots + cats * (UNROLL - 1)
        self.length = (self.length + UNROLL - 1) // UNROLL * UNROLL

    def bounds(self, list_ref, lo, hi):
        return list_ref[self.length + lo], list_ref[self.length + hi]


def prep_body(plan, pad_col, me_ref, cnt_ref, rows_ref, cols_ref, list_ref):
    me = me_ref[0]
    cats, blocks_dev = plan.cats, plan.blocks_dev
    pad = (blocks_dev << 8) | (pad_col << 16)
    live = cnt_ref[0]

    def category(col):
        if cats == 1:
            return 0, col
        return lax.bitwise_xor(col // blocks_dev, me) * 8, lax.rem(col, blocks_dev)

    def count(s, total):
        return total + (1 << category(cols_ref[s])[0])

    total = lax.fori_loop(0, live, count, jnp.int32(0))
    group = jnp.int32(0)
    places = jnp.int32(0)
    for k in range(cats):
        n = (total >> (8 * k)) & 255
        list_ref[plan.length + k] = group
        places = places + ((group * UNROLL) << (8 * k))
        group = group + (n + UNROLL - 1) // UNROLL
        for u in range(1, UNROLL):
            list_ref[lax.max(group * UNROLL - u, 0)] = pad
    list_ref[plan.length + cats] = group
    list_ref[plan.length + cats + 1] = me if cats > 1 else 0

    def place(s, places):
        shift, local = category(cols_ref[s])
        list_ref[(places >> shift) & 255] = s | (rows_ref[s] << 8) | (local << 16)
        return places + (1 << shift)

    lax.fori_loop(0, live, place, places)


def prepare(plan, pad_col, me, info):
    return pl.pallas_call(
        functools.partial(prep_body, plan, pad_col),
        out_shape=pltpu.SMEM((plan.length + plan.cats + 2,), jnp.int32),
        in_specs=[SMEM] * 4,
        out_specs=SMEM,
    )(me.reshape(1), *info)


def tile_of(e):
    return e & 255


def row_of(e):
    return (e >> 8) & 255


def col_of(e):
    return e >> 16


def rows_at(block):
    return pl.ds(pl.multiple_of(block * TILE, TILE), TILE)


def tie(x, *others):
    return lax.optimization_barrier((x, *others))[0]


def join(*xs):
    return lax.optimization_barrier(xs)


def move(x):
    def body(x_ref, out_ref, sem):
        copy = pltpu.make_async_copy(x_ref, out_ref, sem)
        copy.start()
        copy.wait()

    return pl.pallas_call(
        body,
        out_shape=jax.ShapeDtypeStruct(x.shape, x.dtype),
        in_specs=[VMEM],
        out_specs=pl.BlockSpec(memory_space=pl.ANY),
        scratch_shapes=[pltpu.SemaphoreType.DMA],
        cost_estimate=pl.CostEstimate(flops=0, bytes_accessed=1024, transcendentals=0),
        compiler_params=params(4),
    )(x)


def add_rows(total, *parts):
    shape = parts[0].shape

    def body(*refs):
        out_ref = refs[-1]
        acc = refs[0][0:shape[0], :]
        for ref in refs[1:-1]:
            acc = acc + ref[...].astype(F32)
        out_ref[...] = acc.astype(BF16)

    return pl.pallas_call(
        body,
        out_shape=jax.ShapeDtypeStruct(shape, BF16),
        in_specs=[VMEM] * (1 + len(parts)),
        out_specs=VMEM,
        cost_estimate=pl.CostEstimate(flops=0, bytes_accessed=1024, transcendentals=0),
        compiler_params=params(8),
    )(total, *parts)


def forward_groups(list_ref, bounds, tiles_ref, x_ref, acc):
    last = x_ref.shape[0] // TILE - 1

    def step(g, carry):
        es = [list_ref[g * UNROLL + u] for u in range(UNROLL)]
        ds = [
            jnp.dot(
                tiles_ref[tile_of(e)],
                x_ref[rows_at(lax.min(col_of(e), last)), :],
                preferred_element_type=F32,
            )
            for e in es
        ]
        for e, d in zip(es, ds):
            acc[row_of(e)] += d
        return carry

    lax.fori_loop(*bounds, step, 0)


def backward_groups(list_ref, bounds, tiles_ref, s_ref, acc):
    last = s_ref.shape[0] // TILE - 1

    def step(g, carry):
        es = [list_ref[g * UNROLL + u] for u in range(UNROLL)]
        ds = [
            lax.dot_general(
                tiles_ref[tile_of(e)],
                s_ref[rows_at(lax.min(row_of(e), last)), :],
                (((0,), (0,)), ((), ())),
                preferred_element_type=F32,
            )
            for e in es
        ]
        for e, d in zip(es, ds):
            acc[col_of(e)] += d
        return carry

    lax.fori_loop(*bounds, step, 0)


def forward_body(plan, phases, final, first, refs):
    refs = list(refs)
    list_ref, tiles_ref = refs[:2]
    xs = refs[2:2 + len(phases)]
    refs = refs[2 + len(phases):]
    blocks_dev = plan.blocks_dev
    if not first:
        acc_in = refs.pop(0)
    if final:
        w_ref, cot_ref, act_ref, sw_ref, keep_ref, send_ref, acc, wg = refs
    else:
        (acc,) = refs
    if first:
        acc[...] = jnp.zeros_like(acc)
    else:
        acc[0:blocks_dev] = acc_in[0:blocks_dev]
    for k, x_ref in zip(phases, xs):
        forward_groups(list_ref, plan.bounds(list_ref, k, k + 1), tiles_ref, x_ref, acc)
    if not final:
        return
    hid = w_ref.shape[0]
    w = w_ref[...]
    step_blocks = blocks_dev
    n = step_blocks * TILE
    for b in range(0, blocks_dev, step_blocks):
        at = slice(b * TILE, b * TILE + n)
        agg = acc[b:b + step_blocks].reshape(n, hid).astype(BF16)
        pre = jnp.dot(agg, w, preferred_element_type=F32)
        sig = 0.5 + 0.5 * jnp.tanh(0.5 * pre)
        act_ref[at, :] = (pre * sig).astype(BF16)
        slope = (cot_ref[at, :].astype(F32) * sig * (1.0 + pre * (1.0 - sig))).astype(BF16)
        sw_ref[at, :] = lax.dot_general(
            slope, w, (((1,), (1,)), ((), ())), preferred_element_type=F32
        ).astype(BF16)
        part = lax.dot_general(agg, slope, (((0,), (0,)), ((), ())), preferred_element_type=F32)
        if b == 0:
            wg[...] = part
        else:
            wg[...] += part
    rows = keep_ref.shape[0]
    core = list_ref[plan.length + plan.cats + 1] & 1
    keep_ref[...] = wg[pl.ds(pl.multiple_of(core * rows, rows), rows), :]
    send = wg[pl.ds(pl.multiple_of((1 - core) * rows, rows), rows), :]
    send_ref[...] = send.astype(send_ref.dtype)


def forward(plan, lst, tiles, xs, phases, acc=None, tail=None):
    hid = xs[0].shape[1]
    blocks_dev = plan.blocks_dev
    first, final = acc is None, tail is not None
    args = [lst, tiles, *xs] + ([] if first else [acc])
    specs = [SMEM] + [VMEM] * (len(args) - 1)
    scratch = []
    if final:
        scratch.append(pltpu.VMEM((blocks_dev + 1, TILE, hid), F32))
        args += list(tail)
        specs += [VMEM, VMEM]
        out = (
            pltpu.VMEM((blocks_dev * TILE, hid), BF16),
            jax.ShapeDtypeStruct((blocks_dev * TILE, hid), BF16),
            jax.ShapeDtypeStruct((hid // 2, hid), F32),
            jax.ShapeDtypeStruct((hid // 2, hid), BF16 if plan.cats > 1 else F32),
        )
        out_specs = (VMEM,) * 4
        scratch.append(pltpu.VMEM((hid, hid), F32))
    else:
        out = jax.ShapeDtypeStruct((blocks_dev + 1, TILE, hid), F32)
        out_specs = VMEM

    def body(*refs):
        forward_body(plan, phases, final, first, refs)

    return pl.pallas_call(
        body,
        out_shape=out,
        in_specs=specs,
        out_specs=out_specs,
        scratch_shapes=scratch,
        compiler_params=params(12),
    )(*args)


def backward(plan, lst, rel, tiles, s, blocks, rounded=True, us=0):
    hid = s.shape[1]

    def body(list_ref, tiles_ref, s_ref, out_ref, acc=None):
        acc = acc if rounded else out_ref
        acc[...] = jnp.zeros_like(acc)
        bounds = plan.bounds(list_ref, rel, rel + 1)
        backward_groups(list_ref, bounds, tiles_ref, s_ref, acc)
        if rounded:
            out_ref[...] = acc[0:blocks].reshape(blocks * TILE, hid).astype(BF16)

    shape = (blocks + 1, TILE, hid)
    out = pl.pallas_call(
        body,
        out_shape=jax.ShapeDtypeStruct(
            (blocks * TILE, hid) if rounded else shape, BF16 if rounded else F32
        ),
        in_specs=[SMEM, VMEM, VMEM],
        out_specs=VMEM,
        scratch_shapes=[pltpu.VMEM(shape, F32)] if rounded else [],
        compiler_params=params(40 if blocks > 8 else 12),
        cost_estimate=pl.CostEstimate(
            flops=int(us * 1.1e9), bytes_accessed=1024, transcendentals=0
        ),
    )(lst, tiles, s)
    return out if rounded else out.reshape(-1, hid)


def local_four(features, weight, cotangent, tiles, tile_rows, tile_cols, tile_counts):
    blocks_dev = features.shape[0] // TILE
    me = lax.axis_index("grp").astype(jnp.int32)
    core = lax.bitwise_and(me, 1)

    def swap(x, bit):
        return lax.ppermute(x, "grp", [(i, i ^ bit) for i in range(4)])

    def fold(w, axis, size, bit, *others):
        other = lax.ppermute(w, axis, [(i, i ^ bit) for i in range(size)])
        if others:
            other = tie(other, *others)
        return (w.astype(F32) + other.astype(F32)).astype(BF16)

    far = swap(features, 2)
    sib = swap(features, 1)
    plan = Plan(tile_rows.shape[0], 4, blocks_dev)
    lst = prepare(plan, blocks_dev, me, [tile_counts, tile_rows, tile_cols])
    acc = forward(plan, lst, tiles, [features, sib], [0, 1])
    far, acc = join(far, acc)
    diag = swap(far, 1)
    acc = forward(plan, lst, tiles, [far], [2], acc)
    activated, sw, keep, send = forward(
        plan, lst, tiles, [diag], [3], acc, (weight, cotangent)
    )

    def part(rel, sw, rounded=True, us=0):
        return backward(plan, lst, rel, tiles, sw, blocks_dev, rounded, us)

    send = swap(send, 1)
    p3 = part(3, sw)
    r3 = swap(p3, 1)
    w = (keep + send.astype(F32)).astype(BF16)
    q = part(2, tie(sw, w), False, 10)
    q = add_rows(q, r3)
    q_far = swap(q, 2)
    w = fold(w, "grp", 4, 2, q)
    p1 = part(1, tie(sw, w))
    w = fold(w, "row", 8, 1, p1)
    r1 = swap(tie(p1, w), 1)
    p0 = part(0, tie(sw, w), False)
    w = fold(w, "row", 8, 2, p0)
    activated = move(tie(activated, w))
    feature_grad = add_rows(p0, r1, q_far)
    w = fold(w, "row", 8, 4, activated, feature_grad)
    other = swap(w, 1)
    weight_grad = jnp.where(
        core == 0, jnp.concatenate([w, other]), jnp.concatenate([other, w])
    ).astype(F32)
    return activated, feature_grad, weight_grad


def local_any(features, weight, cotangent, tiles, tile_rows, tile_cols, tile_counts):
    blocks_dev = features.shape[0] // TILE
    group_blocks = blocks_dev * lax.axis_size("grp")
    me = lax.axis_index("grp").astype(jnp.int32)
    panel = lax.all_gather(features, "grp", axis=0, tiled=True)
    info = [tile_counts, tile_rows, tile_cols]
    plan = Plan(tile_rows.shape[0], 1, blocks_dev)
    lst = prepare(plan, group_blocks, me, info)
    activated, sw, keep, send = forward(
        plan, lst, tiles, [panel], [0], None, (weight, cotangent)
    )
    partial = backward(plan, lst, 0, tiles, sw, group_blocks)
    feature_grad = lax.psum_scatter(partial, "grp", scatter_dimension=0, tiled=True)
    weight_grad = lax.psum(jnp.concatenate([keep, send]), ("row", "grp"))
    return activated, feature_grad, weight_grad


def solution(mesh):
    split = P(("row", "grp"))
    four = mesh.shape["grp"] == 4 and mesh.shape["row"] == 8
    return jax.shard_map(
        local_four if four else local_any,
        mesh=mesh,
        in_specs=(split, P(), split, split, split, split, split),
        out_specs=(split, split, P()),
        check_vma=False,
    )
```
